512 devices in a mesh: pool: 32 (over x, y), head: 16 (over z, core).
Axes of the slice: x: 4, y: 8, z: 8, core: 2. Of those that a mesh axis runs over, the one named last changes fastest.
Arguments:
- queries: bfloat16 [1024, 8192], P('pool', 'head'), may hold values from -120 to 120, as said below
- branch_prefix: int32 [1024], replicated, may hold values from 0 to 15
- stretch_table: int32 [256], P('pool'), may hold values from 0 to 255, each once
- suffix_len: int32 [1024], P('pool'), may hold values from 1 to 128, 65536 in all
- prefix_keys: bfloat16 [16, 32768, 128], P('head', 'pool'), may hold values from -4 to 4, as said below
- prefix_values: bfloat16 [16, 32768, 128], P('head', 'pool'), may hold values from -4 to 4, as said below
- suffix_keys: bfloat16 [16, 1024, 128, 128], P('head', 'pool'), may hold values from -4 to 4, as said below
- suffix_values: bfloat16 [16, 1024, 128, 128], P('head', 'pool'), may hold values from -4 to 4, as said below
- out_weight: bfloat16 [8192, 8192], P('head', 'pool'), may hold values from -0.14941406 to 0.14941406
Outputs:
- mixed: bfloat16 [1024, 8192], P('head', 'pool')
The draws below stay inside these ranges and needn't reach their ends.
Inputs may be any that keep to these rules, and one draw needn't show every extreme that they name: `queries`: row b holds branch b's 64 query heads in order, 128 entries each. `branch_prefix`: the prefix that each branch extends. Slot s holds block stretch_table[s] % 16 of prefix stretch_table[s] // 16; each value appears once. `suffix_len`: counts the branch's own new key; some branch has 128. `prefix_keys`: stored head h is key-value head h * 8 // 16 of the model; copies of one head are equal. `prefix_values`: stored head h is key-value head h * 8 // 16 of the model; copies of one head are equal. `suffix_keys`: stored head h is key-value head h * 8 // 16 of the model; copies of one head are equal. `suffix_values`: stored head h is key-value head h * 8 // 16 of the model; copies of one head are equal.
All inputs are finite; a program needn't handle non-finite values. No bound on the sum of `suffix_len` on one device may be relied on, other than what follows from the above.
Results may differ from the reference program's by a relative error of at most 0.0051.
Values may be sent and summed in bfloat16 or wider, within the bound.
No kernel may reach another device: no remote copies, remote signals or barrier semaphores. Data moves between devices by JAX's collectives and lax.ppermute only.
A program may use at most 64 MiB of HBM per device.

```python
import math
import jax
import jax.numpy as jnp
import numpy as np
from jax import lax

D = 8192
QH = 64
KVH = 8
HD = 128
SLOT_DEV = 8
CH = 128
CPP = 16
SUF = 128
BRANCHES = 1024
KVG = 16
NCHUNK = 256
NPRE = 16
PTOK = 32768
N_POOL = 32


def clipped_normal(key, shape, limit):
    return jnp.clip(jax.random.normal(key, shape, jnp.float32), -limit, limit)


def head_copies(base):
    index = jnp.arange(KVG) * KVH // KVG
    return jnp.take(base, index, axis=0)


def first_keys(key):
    return clipped_normal(jax.random.fold_in(key, 77), (KVH, BRANCHES, 2, HD), 4.0)


def draw_queries(key, part):
    key = jax.random.fold_in(key, 5)
    base = 2.0 * clipped_normal(key, (BRANCHES, QH, HD), 4.0)
    return base.reshape(BRANCHES, QH * HD).astype(jnp.bfloat16)


def draw_suffix_keys(key, part):
    first = first_keys(key)
    key = jax.random.fold_in(key, 3)
    remainder = clipped_normal(key, (KVH, BRANCHES, SUF - 2, HD), 4.0)
    return head_copies(jnp.concatenate([first, remainder], axis=2)).astype(jnp.bfloat16)


def draw_suffix_values(key, part):
    key = jax.random.fold_in(key, 11)
    base = clipped_normal(key, (KVH, BRANCHES, SUF, HD), 4.0)
    return head_copies(base).astype(jnp.bfloat16)


def draw_prefix_keys(key, part):
    key = jax.random.fold_in(key, 7)
    base = clipped_normal(key, (KVH, PTOK, HD), 4.0)
    return head_copies(base).astype(jnp.bfloat16)


def draw_prefix_values(key, part):
    key = jax.random.fold_in(key, 9)
    base = clipped_normal(key, (KVH, PTOK, HD), 4.0)
    return head_copies(base).astype(jnp.bfloat16)


def touch_ends(values, own_key, low, largest):
    longest = values.shape.index(max(values.shape))
    spots = []
    for shift in (0, 1):
        where = [jax.random.randint(jax.random.fold_in(own_key, axis), (), 0, length) for axis, length in enumerate(values.shape)]
        where[longest] = (where[longest] + shift) % values.shape[longest]
        spots.append(tuple(where))
    return values.at[spots[0]].set(low).at[spots[1]].set(largest)


def block_scale(rng, extent, cuts, smallest, high):
    level = 1.0
    for position, blocks in cuts:
        heights = jax.random.uniform(jax.random.fold_in(jax.random.fold_in(rng, 6), position), (blocks,), jnp.float32, smallest / len(cuts), high / len(cuts))
        level = level * jnp.repeat(jnp.exp(heights), extent[position] // blocks).reshape((-1,) + (1,) * (len(extent) - 1 - position))
    return level


def rank_bounds(number_of, skew):
    weights = [(1 << 20) // math.isqrt(grade ** skew) + 1 for grade in range(1, number_of + 1)]
    deviation = 1 + sum(weights) // (1 << 30)
    return np.cumsum(np.array([max(1, weight // deviation) for weight in weights]))


def ranked_ids(key, dims, count, lean):
    grid = rank_bounds(count, lean)
    pick = jax.random.randint(jax.random.fold_in(key, 1), dims, 0, int(grid[count - 1]))
    rank = jnp.searchsorted(jnp.asarray(grid, jnp.int32), pick, side="right")
    return jax.random.permutation(jax.random.fold_in(key, 2), count)[rank].astype(jnp.int32)


def length_profile(count, total, most, slope):
    loads = [(1 << 20) // math.isqrt(rank ** slope) + 1 for rank in range(2, count + 1)]
    spare, counts = total - most - (count - 1), [1] * (count - 1)
    while spare > 0:
        movable = [i for i in range(count - 1) if counts[i] < most]
        whole, remaining = sum([loads[i] for i in movable]), spare
        for i in movable:
            extra = min(most - counts[i], max(1, remaining * loads[i] // whole), spare)
            counts[i] = counts[i] + extra
            spare = spare - extra
    return np.array([most] + counts)


def ragged_sizes(key, number_of, total, bound, skew):
    if number_of == 2:
        one = jax.random.randint(key, (), max(1, total - bound), min(bound, total - 1) + 1)
        return jnp.stack([one, total - one])
    lengths = jnp.asarray(length_profile(number_of, total, bound, skew), jnp.int32)
    twos = (number_of - 1) // 2
    giver, taker = lengths[1:1 + 2 * twos:2], lengths[2:2 + 2 * twos:2]
    slack = jnp.minimum(giver - 1, bound - taker)
    passed = jax.random.randint(jax.random.fold_in(key, 1), (twos,), 0, 1 << 20) % (slack + 1)
    lengths = lengths.at[1:1 + 2 * twos:2].set(giver - passed).at[2:2 + 2 * twos:2].set(taker + passed)
    return lengths[jax.random.permutation(jax.random.fold_in(key, 2), number_of)]


def gaussian(rng, extent, scale, most, split=(), held_as=jnp.bfloat16):
    loudness = block_scale(rng, extent, split, -0.22, 0.18) if split else 1.0
    drawn = jax.random.normal(rng, extent, jnp.float32) * scale * loudness
    return jnp.minimum(jnp.maximum(drawn, -most), most).astype(held_as)


def setup_inputs(seed: int = 0) -> dict:
    arg_keys = jax.random.split(jax.random.key(seed), 10)
    queries = draw_queries(jax.random.fold_in(arg_keys[9], 71), 0)
    branch_prefix = touch_ends(ranked_ids(arg_keys[1], (BRANCHES,), NPRE, 2), jax.random.fold_in(arg_keys[1], 3), 0, NPRE - 1).astype(jnp.int32)
    stretch_table = jax.random.permutation(arg_keys[2], NCHUNK).astype(jnp.int32)
    suffix_len = ragged_sizes(arg_keys[3], BRANCHES, BRANCHES * SUF // 2, SUF, 1).astype(jnp.int32)
    prefix_keys = draw_prefix_keys(jax.random.fold_in(arg_keys[9], 71), 0)
    prefix_values = draw_prefix_values(jax.random.fold_in(arg_keys[9], 71), 0)
    suffix_keys = draw_suffix_keys(jax.random.fold_in(arg_keys[9], 71), 0)
    suffix_values = draw_suffix_values(jax.random.fold_in(arg_keys[9], 71), 0)
    out_weight = gaussian(arg_keys[8], (QH * HD, D), 0.025, 0.14941406, ((0, 16), (1, 32)))
    return {"queries": queries, "branch_prefix": branch_prefix, "stretch_table": stretch_table, "suffix_len": suffix_len, "prefix_keys": prefix_keys, "prefix_values": prefix_values, "suffix_keys": suffix_keys, "suffix_values": suffix_values, "out_weight": out_weight}


masked_score = -1e+30

def join_partials(left, right):
    high_left, totals_left, numer_left = left
    high_right, totals_right, numer_right = right
    highest = jnp.maximum(high_left, high_right)
    factor_left = jnp.exp(high_left - highest)
    factor_right = jnp.exp(high_right - highest)
    totals = totals_left * factor_left + totals_right * factor_right
    numerator = numer_left * factor_left[..., None] + numer_right * factor_right[..., None]
    return (highest, totals, numerator)

def group_partial(query_slot, key_slot, value_slot, visible, form_scores, form_values):
    scores = jnp.einsum(form_scores, query_slot, key_slot.astype(jnp.float32), precision=lax.Precision.HIGHEST) / math.sqrt(HD)
    scores = jnp.where(visible, scores, masked_score)
    highest = lax.optimization_barrier(jnp.max(scores, axis=-1))
    weights = jnp.where(visible, jnp.exp(scores - highest[..., None]), 0.0)
    totals = lax.optimization_barrier(jnp.sum(weights, axis=-1))
    rounded = lax.optimization_barrier(weights.astype(jnp.bfloat16)).astype(jnp.float32)
    numerator = jnp.einsum(form_values, rounded, value_slot.astype(jnp.float32), precision=lax.Precision.HIGHEST)
    return (highest, totals, numerator)

def reference(queries, branch_prefix, stretch_table, suffix_len, prefix_keys, prefix_values, suffix_keys, suffix_values, out_weight):
    group_size = QH // KVG
    local_tokens = SLOT_DEV * CH
    query_all = queries.astype(jnp.float32).reshape(BRANCHES, KVG, group_size, HD)
    query_slots = jnp.transpose(query_all, (1, 0, 2, 3))
    token_prefix = jnp.repeat(stretch_table // CPP, CH)
    visible_suffix = (jnp.arange(SUF, dtype=jnp.int32)[None, :] < suffix_len[:, None])[:, None, :]

    def suffix_slot(operands):
        query_slot, key_slot, value_slot = operands
        return group_partial(query_slot, key_slot, value_slot, visible_suffix, 'bgd,btd->bgt', 'bgt,btd->bgd')
    suffix_part = lax.map(suffix_slot, (query_slots, suffix_keys, suffix_values))

    def owner_step(carry, owner):
        first_token = (owner * local_tokens).astype(jnp.int32)
        keys = lax.dynamic_slice_in_dim(prefix_keys, first_token, local_tokens, 1)
        values = lax.dynamic_slice_in_dim(prefix_values, first_token, local_tokens, 1)
        prefixes = lax.dynamic_slice_in_dim(token_prefix, first_token, local_tokens, 0)
        visible = (branch_prefix[:, None] == prefixes[None, :])[:, None, :]

        def prefix_slot(operands):
            query_slot, key_slot, value_slot = operands
            return group_partial(query_slot, key_slot, value_slot, visible, 'bgd,td->bgt', 'bgt,td->bgd')
        part = lax.map(prefix_slot, (query_slots, keys, values))
        return (join_partials(carry, part), None)
    start_state = (jnp.full((KVG, BRANCHES, group_size), masked_score, jnp.float32), jnp.zeros((KVG, BRANCHES, group_size), jnp.float32), jnp.zeros((KVG, BRANCHES, group_size, HD), jnp.float32))
    prefix_part, unused = lax.scan(owner_step, start_state, jnp.arange(N_POOL, dtype=jnp.int32))
    highest, totals, numerator = join_partials(suffix_part, prefix_part)
    attention = numerator / totals[..., None]
    attention = jnp.transpose(attention, (1, 0, 2, 3)).reshape(BRANCHES, QH * HD).astype(jnp.bfloat16)
    return jnp.dot(attention, out_weight, preferred_element_type=jnp.float32).astype(jnp.bfloat16)
```

```python
import math

import jax
import jax.numpy as jnp
from jax import lax
from jax.experimental import pallas as pl
from jax.experimental.pallas import tpu as pltpu
from jax.sharding import PartitionSpec as P

CPP = 16
NX, NY = 4, 8
HEADS = 4
HD = 128
ROWS = 32
MEMBERS = 16
LANES = 128
TAB = 16
HIDE = -1e30
FLOOR = -262144.0
LOG2E = 1.4426950408889634
SCALE = LOG2E / math.sqrt(HD)
f32, bf16 = jnp.float32, jnp.bfloat16

GROUP_X = ((0, 3), (1, 2))
GROUPS = [[x * NY + y for x in xs for y in range(NY)] for xs in GROUP_X]
PAIR = [(x * NY + y, (x ^ 1) * NY + y) for x in range(NX) for y in range(NY)]


def nt_dot(a, b):
    return lax.dot_general(a, b, (((1,), (1,)), ((), ())), preferred_element_type=f32)


def suffix_kernel(q_ref, len_ref, k_ref, v_ref, numer_ref, stat_ref):
    rows = HEADS * ROWS
    q = jnp.concatenate([q_ref[:, j * HD : (j + 1) * HD] for j in range(HEADS)], axis=0)
    row = lax.broadcasted_iota(jnp.int32, (rows, LANES), 0) % ROWS
    lane = lax.broadcasted_iota(jnp.int32, (rows, LANES), 1)
    live = lane < jnp.concatenate([len_ref[...]] * HEADS, axis=0)
    picked = jnp.full((rows, LANES), HIDE, f32)
    for b in range(ROWS):
        picked = jnp.where(row == b, nt_dot(q, k_ref[b]), picked)
    picked = jnp.where(live, picked, HIDE)
    high = jnp.max(picked, axis=1, keepdims=True)
    weights = jnp.exp2((picked - high) * SCALE)
    totals = jnp.sum(weights, axis=1, keepdims=True)
    rounded = weights.astype(bf16)
    zero = jnp.zeros((rows, LANES), bf16)
    acc = jnp.zeros((rows, HD), f32)
    for b in range(0, ROWS, 2):
        w = jnp.concatenate(
            [jnp.where(row == b, weights, 0.0).astype(bf16), jnp.where(row == b + 1, weights, 0.0).astype(bf16)],
            axis=1,
        )
        v = jnp.concatenate([v_ref[b], v_ref[b + 1]], axis=0)
        acc = acc + jnp.dot(w, v, preferred_element_type=f32)
    for j in range(HEADS):
        numer_ref[:, j * HD : (j + 1) * HD] = acc[j * ROWS : (j + 1) * ROWS]
    lane = lax.broadcasted_iota(jnp.int32, (ROWS, LANES), 1)
    stat = jnp.zeros((ROWS, LANES), f32)
    for j in range(HEADS):
        part = slice(j * ROWS, (j + 1) * ROWS)
        stat = jnp.where(lane == j, high[part] * SCALE, stat)
        stat = jnp.where(lane == HEADS + j, totals[part], stat)
    stat_ref[...] = stat


def owner_kernel(q_ref, hide_ref, own_ref, oth_ref, out_ref, keys_ref):
    tokens = (own_ref.shape[0] - TAB) // 2
    slots = tokens // LANES
    lane = lax.broadcasted_iota(jnp.int32, (LANES, LANES), 1)
    for o, ref in enumerate((own_ref, oth_ref)):
        table = ref[2 * tokens : 2 * tokens + TAB, :].astype(f32)
        keys_ref[o, :, :HD] = ref[:tokens, :]
        for s in range(slots):
            other = (lane < CPP) & (lane.astype(f32) != table[0:1, s : s + 1])
            keys_ref[o, s * LANES : (s + 1) * LANES, HD:] = jnp.where(other, 1.0, 0.0).astype(bf16)
    branches = MEMBERS * ROWS
    block = 256
    lane = lax.broadcasted_iota(jnp.int32, (block, LANES), 1)
    per = block // ROWS
    for r in range(branches // block):
        hide = hide_ref[r * block : (r + 1) * block, :]
        stat = jnp.zeros((block, LANES), f32)
        for j in range(HEADS):
            q = q_ref[r * per : (r + 1) * per, :, j * HD : (j + 1) * HD].reshape(block, HD)
            q = jnp.concatenate([q, hide], axis=1)
            parts = []
            for o, ref in enumerate((own_ref, oth_ref)):
                scores = nt_dot(q, keys_ref[o])
                high = jnp.maximum(jnp.max(scores, axis=1, keepdims=True), FLOOR)
                weights = jnp.exp2((scores - high) * SCALE)
                totals = jnp.sum(weights, axis=1, keepdims=True)
                numer = jnp.dot(weights.astype(bf16), ref[tokens : 2 * tokens, :], preferred_element_type=f32)
                parts.append((high * SCALE, totals, numer))
            (ha, ta, na), (hb, tb, nb) = parts
            high = jnp.maximum(ha, hb).astype(bf16).astype(f32)
            fa, fb = jnp.exp2(ha - high), jnp.exp2(hb - high)
            numer = na * fa + nb * fb
            totals = ta * fa + tb * fb
            coarse = totals.astype(bf16).astype(f32)
            out_ref[r * per : (r + 1) * per, :, j * HD : (j + 1) * HD] = numer.astype(bf16).reshape(per, ROWS, HD)
            stat = jnp.where(lane == j, high, stat)
            stat = jnp.where(lane == HEADS + j, coarse, stat)
            stat = jnp.where(lane == 2 * HEADS + j, totals - coarse, stat)
        out_ref[r * per : (r + 1) * per, :, HEADS * HD :] = stat.astype(bf16).reshape(per, ROWS, LANES)


def join_kernel(got_ref, numer_ref, stat_ref, out_ref):
    wide = HEADS * HD
    own = stat_ref[...]
    top = own
    for i in range(MEMBERS):
        top = jnp.maximum(top, got_ref[i, :, wide:].astype(f32))
    lane = lax.broadcasted_iota(jnp.int32, (ROWS, LANES), 1)
    shift = lane < HEADS
    top = jnp.where(shift, top, 0.0)
    fac_own = jnp.exp2(jnp.where(shift, own, 0.0) - top)
    numer = [numer_ref[:, j * HD : (j + 1) * HD] * fac_own[:, j : j + 1] for j in range(HEADS)]
    total = [own[:, HEADS + j : HEADS + j + 1] * fac_own[:, j : j + 1] for j in range(HEADS)]
    for i in range(MEMBERS):
        stat = got_ref[i, :, wide:].astype(f32)
        fac = jnp.exp2(jnp.where(shift, stat, 0.0) - top)
        for j in range(HEADS):
            f = fac[:, j : j + 1]
            numer[j] = numer[j] + got_ref[i, :, j * HD : (j + 1) * HD].astype(f32) * f
            t = stat[:, HEADS + j : HEADS + j + 1] + stat[:, 2 * HEADS + j : 2 * HEADS + j + 1]
            total[j] = total[j] + t * f
    for j in range(HEADS):
        out_ref[:, j * HD : (j + 1) * HD] = (numer[j] / total[j]).astype(bf16)


def project_kernel(att_ref, w_ref, out_ref):
    depth = att_ref.shape[2]
    half = att_ref.shape[0] // 2
    acc = jnp.zeros(out_ref.shape, f32)
    for h in range(half):
        rows = jnp.concatenate([att_ref[h], att_ref[half + h]], axis=0)
        acc = acc + jnp.dot(rows, w_ref[h * depth : (h + 1) * depth, :], preferred_element_type=f32)
    out_ref[...] = acc.astype(bf16)


def call(kernel, out_shape, *args, flops=0, moved=0, scratch=()):
    return pl.pallas_call(
        kernel,
        out_shape=out_shape,
        scratch_shapes=scratch,
        compiler_params=pltpu.CompilerParams(vmem_limit_bytes=40 * 2**20),
        cost_estimate=pl.CostEstimate(flops=flops, bytes_accessed=moved, transcendentals=0),
    )(*args)


def on_device(
    queries,
    branch_prefix,
    stretch_table,
    suffix_len,
    prefix_keys,
    prefix_values,
    suffix_keys,
    suffix_values,
    out_weight,
):
    pool = lax.axis_index("pool")
    x = pool // NY
    slots = stretch_table.shape[0]

    prefixes = (stretch_table // CPP).astype(bf16)
    table = jnp.zeros((TAB, LANES), bf16).at[0, :slots].set(prefixes)
    own = jnp.concatenate([prefix_keys[0], prefix_values[0], table], axis=0)
    oth = lax.ppermute(own, "pool", PAIR)

    weight = lax.all_gather(out_weight, "head", axis=0, tiled=True)

    got = lax.all_to_all(
        jnp.broadcast_to(queries[None], (MEMBERS,) + queries.shape),
        "pool",
        split_axis=0,
        concat_axis=0,
        tiled=True,
        axis_index_groups=GROUPS,
    )
    span = NY * ROWS
    outer = (x == GROUP_X[0][0]) | (x == GROUP_X[0][1])
    mine = jnp.where(
        outer,
        jnp.concatenate([branch_prefix[xx * span : (xx + 1) * span] for xx in GROUP_X[0]]),
        jnp.concatenate([branch_prefix[xx * span : (xx + 1) * span] for xx in GROUP_X[1]]),
    )
    hide = jnp.where(mine[:, None] == jnp.arange(LANES, dtype=jnp.int32)[None, :], HIDE, 0.0).astype(bf16)

    suffix_numer, suffix_stat = call(
        suffix_kernel,
        (
            jax.ShapeDtypeStruct((ROWS, HEADS * HD), f32),
            jax.ShapeDtypeStruct((ROWS, LANES), f32),
        ),
        queries,
        suffix_len[:, None],
        suffix_keys[0],
        suffix_values[0],
        flops=2 * 2 * 128 * 128 * 4096,
        moved=2 * 2**20,
    )

    state = call(
        owner_kernel,
        jax.ShapeDtypeStruct((MEMBERS, ROWS, HEADS * HD + LANES), bf16),
        got,
        hide,
        own,
        oth,
        flops=4 * 2048 * 2048 * 128,
        moved=2 * 2**20,
        scratch=[pltpu.VMEM((2, prefix_keys.shape[1], 2 * HD), bf16)],
    )
    state = lax.all_to_all(
        state, "pool", split_axis=0, concat_axis=0, tiled=True, axis_index_groups=GROUPS
    )
    attention = call(
        join_kernel,
        jax.ShapeDtypeStruct((ROWS, HEADS * HD), bf16),
        state,
        suffix_numer,
        suffix_stat,
        flops=2**21,
        moved=2**20,
    )

    heads = lax.axis_size("head")
    moves = [
        (p * heads + h, ((p % 2) * heads + h) * heads + p // 2)
        for p in range(NX * NY)
        for h in range(heads)
    ]
    attention = lax.ppermute(attention, ("pool", "head"), moves)
    everything = lax.all_to_all(
        jnp.broadcast_to(attention[None], (NX * NY,) + attention.shape),
        "pool",
        split_axis=0,
        concat_axis=0,
        tiled=True,
    )
    return call(
        project_kernel,
        jax.ShapeDtypeStruct((2 * ROWS, out_weight.shape[1]), bf16),
        everything,
        weight,
        flops=2 * 64 * 8192 * 256,
        moved=5 * 2**20,
    )


def solution(mesh):
    in_specs = (
        P("pool", "head"),
        P(),
        P("pool"),
        P("pool"),
        P("head", "pool", None),
        P("head", "pool", None),
        P("head", "pool", None, None),
        P("head", "pool", None, None),
        P("head", "pool"),
    )
    out_specs = P("head", "pool")
    return jax.shard_map(
        on_device, mesh=mesh, in_specs=in_specs, out_specs=out_specs, check_vma=False
    )
```

```python
import math

import jax
import jax.numpy as jnp
from jax import lax
from jax.experimental import pallas as pl
from jax.experimental.pallas import tpu as pltpu
from jax.sharding import PartitionSpec as P

CPP = 16
NX, NY = 4, 8
HEADS = 4
HD = 128
ROWS = 32
MEMBERS = 16
LANES = 128
TAB = 16
HIDE = -1e30
FLOOR = -262144.0
LOG2E = 1.4426950408889634
SCALE = LOG2E / math.sqrt(HD)
f32, bf16 = jnp.float32, jnp.bfloat16

GROUP_X = ((0, 3), (1, 2))
GROUPS = [[x * NY + y for x in xs for y in range(NY)] for xs in GROUP_X]
PAIR = [(x * NY + y, (x ^ 1) * NY + y) for x in range(NX) for y in range(NY)]
X_GROUPS = [[x * NY + y for x in range(NX)] for y in range(NY)]
Y_GROUPS = [[x * NY + y for y in range(NY)] for x in range(NX)]
NH = 16


def place(x, y, h):
    return (x * NY + y) * NH + h


EVERY = [(x, y, h) for x in range(NX) for y in range(NY) for h in range(NH)]
WEIGHT_MOVES = [(place(x, y, h), place(h % NX, y, h - h % NX + x)) for x, y, h in EVERY]
ATTENTION_MOVES = [
    (place(x, y, h), place(h % NX, (y % 2) * NX + h // NX, NX * x + y // 2)) for x, y, h in EVERY
]


def nt_dot(a, b):
    return lax.dot_general(a, b, (((1,), (1,)), ((), ())), preferred_element_type=f32)


def suffix_kernel(q_ref, len_ref, k_ref, v_ref, numer_ref, stat_ref):
    rows = HEADS * ROWS
    q = jnp.concatenate([q_ref[:, j * HD : (j + 1) * HD] for j in range(HEADS)], axis=0)
    row = lax.broadcasted_iota(jnp.int32, (rows, LANES), 0) % ROWS
    lane = lax.broadcasted_iota(jnp.int32, (rows, LANES), 1)
    live = lane < jnp.concatenate([len_ref[...]] * HEADS, axis=0)
    picked = jnp.full((rows, LANES), HIDE, f32)
    for b in range(ROWS):
        picked = jnp.where(row == b, nt_dot(q, k_ref[b]), picked)
    picked = jnp.where(live, picked, HIDE)
    high = jnp.max(picked, axis=1, keepdims=True)
    weights = jnp.exp2((picked - high) * SCALE)
    totals = jnp.sum(weights, axis=1, keepdims=True)
    rounded = weights.astype(bf16)
    zero = jnp.zeros((rows, LANES), bf16)
    acc = jnp.zeros((rows, HD), f32)
    for b in range(0, ROWS, 2):
        w = jnp.concatenate(
            [jnp.where(row == b, weights, 0.0).astype(bf16), jnp.where(row == b + 1, weights, 0.0).astype(bf16)],
            axis=1,
        )
        v = jnp.concatenate([v_ref[b], v_ref[b + 1]], axis=0)
        acc = acc + jnp.dot(w, v, preferred_element_type=f32)
    for j in range(HEADS):
        numer_ref[:, j * HD : (j + 1) * HD] = acc[j * ROWS : (j + 1) * ROWS]
    lane = lax.broadcasted_iota(jnp.int32, (ROWS, LANES), 1)
    stat = jnp.zeros((ROWS, LANES), f32)
    for j in range(HEADS):
        part = slice(j * ROWS, (j + 1) * ROWS)
        stat = jnp.where(lane == j, high[part] * SCALE, stat)
        stat = jnp.where(lane == HEADS + j, totals[part], stat)
    stat_ref[...] = stat


def owner_kernel(q_ref, hide_ref, own_ref, oth_ref, out_ref, keys_ref):
    tokens = (own_ref.shape[0] - TAB) // 2
    slots = tokens // LANES
    lane = lax.broadcasted_iota(jnp.int32, (LANES, LANES), 1)
    for o, ref in enumerate((own_ref, oth_ref)):
        table = ref[2 * tokens : 2 * tokens + TAB, :].astype(f32)
        keys_ref[o, :, :HD] = ref[:tokens, :]
        for s in range(slots):
            other = (lane < CPP) & (lane.astype(f32) != table[0:1, s : s + 1])
            keys_ref[o, s * LANES : (s + 1) * LANES, HD:] = jnp.where(other, 1.0, 0.0).astype(bf16)
    branches = MEMBERS * ROWS
    block = 512
    lane = lax.broadcasted_iota(jnp.int32, (block, LANES), 1)
    per = block // ROWS
    for r in range(branches // block):
        hide = hide_ref[r * block : (r + 1) * block, :]
        stat = jnp.zeros((block, LANES), f32)
        for j in range(HEADS):
            q = q_ref[r * per : (r + 1) * per, :, j * HD : (j + 1) * HD].reshape(block, HD)
            q = jnp.concatenate([q, hide], axis=1)
            parts = []
            for o, ref in enumerate((own_ref, oth_ref)):
                scores = nt_dot(q, keys_ref[o])
                high = jnp.maximum(jnp.max(scores, axis=1, keepdims=True), FLOOR)
                weights = jnp.exp2((scores - high) * SCALE)
                totals = jnp.sum(weights, axis=1, keepdims=True)
                numer = jnp.dot(weights.astype(bf16), ref[tokens : 2 * tokens, :], preferred_element_type=f32)
                parts.append((high * SCALE, totals, numer))
            (ha, ta, na), (hb, tb, nb) = parts
            high = jnp.maximum(ha, hb).astype(bf16).astype(f32)
            fa, fb = jnp.exp2(ha - high), jnp.exp2(hb - high)
            numer = na * fa + nb * fb
            totals = ta * fa + tb * fb
            coarse = totals.astype(bf16).astype(f32)
            out_ref[r * per : (r + 1) * per, :, j * HD : (j + 1) * HD] = numer.astype(bf16).reshape(per, ROWS, HD)
            stat = jnp.where(lane == j, high, stat)
            stat = jnp.where(lane == HEADS + j, coarse, stat)
            stat = jnp.where(lane == 2 * HEADS + j, totals - coarse, stat)
        out_ref[r * per : (r + 1) * per, :, HEADS * HD :] = stat.astype(bf16).reshape(per, ROWS, LANES)


def join_kernel(got_ref, numer_ref, stat_ref, out_ref):
    wide = HEADS * HD
    own = stat_ref[...]
    top = own
    for i in range(MEMBERS):
        top = jnp.maximum(top, got_ref[i, :, wide:].astype(f32))
    lane = lax.broadcasted_iota(jnp.int32, (ROWS, LANES), 1)
    shift = lane < HEADS
    top = jnp.where(shift, top, 0.0)
    fac_own = jnp.exp2(jnp.where(shift, own, 0.0) - top)
    numer = [numer_ref[:, j * HD : (j + 1) * HD] * fac_own[:, j : j + 1] for j in range(HEADS)]
    total = [own[:, HEADS + j : HEADS + j + 1] * fac_own[:, j : j + 1] for j in range(HEADS)]
    for i in range(MEMBERS):
        stat = got_ref[i, :, wide:].astype(f32)
        fac = jnp.exp2(jnp.where(shift, stat, 0.0) - top)
        for j in range(HEADS):
            f = fac[:, j : j + 1]
            numer[j] = numer[j] + got_ref[i, :, j * HD : (j + 1) * HD].astype(f32) * f
            t = stat[:, HEADS + j : HEADS + j + 1] + stat[:, 2 * HEADS + j : 2 * HEADS + j + 1]
            total[j] = total[j] + t * f
    for j in range(HEADS):
        out_ref[:, j * HD : (j + 1) * HD] = (numer[j] / total[j]).astype(bf16)


def project_kernel(att_ref, w_ref, out_ref):
    depth = att_ref.shape[2]
    half = att_ref.shape[0] // 2
    for c in range(out_ref.shape[0]):
        acc = jnp.zeros(out_ref.shape[1:], f32)
        for k in range(half):
            rows = jnp.concatenate([att_ref[k], att_ref[half + k]], axis=0)
            i = k * out_ref.shape[0] + c
            acc = acc + jnp.dot(rows, w_ref[i * depth : (i + 1) * depth, :], preferred_element_type=f32)
        out_ref[c] = acc.astype(out_ref.dtype)


def sum_kernel(part_ref, out_ref):
    acc = part_ref[0].astype(f32)
    for c in range(1, part_ref.shape[0]):
        acc = acc + part_ref[c].astype(f32)
    out_ref[...] = acc.astype(bf16)


def call(kernel, out_shape, *args, flops=0, moved=0, scratch=()):
    return pl.pallas_call(
        kernel,
        out_shape=out_shape,
        scratch_shapes=scratch,
        compiler_params=pltpu.CompilerParams(vmem_limit_bytes=40 * 2**20),
        cost_estimate=pl.CostEstimate(flops=flops, bytes_accessed=moved, transcendentals=0),
    )(*args)


def after(value, other):
    return lax.optimization_barrier((value, other))[0]


def on_device(
    queries,
    branch_prefix,
    stretch_table,
    suffix_len,
    prefix_keys,
    prefix_values,
    suffix_keys,
    suffix_values,
    out_weight,
):
    pool = lax.axis_index("pool")
    x = pool // NY
    slots = stretch_table.shape[0]

    prefixes = (stretch_table // CPP).astype(bf16)
    table = jnp.zeros((TAB, LANES), bf16).at[0, :slots].set(prefixes)
    own = jnp.concatenate([prefix_keys[0], prefix_values[0], table], axis=0)
    oth = lax.ppermute(own, "pool", PAIR)

    got = lax.all_to_all(
        jnp.broadcast_to(queries[None], (MEMBERS,) + queries.shape),
        "pool",
        split_axis=0,
        concat_axis=0,
        tiled=True,
        axis_index_groups=GROUPS,
    )
    weight = lax.ppermute(out_weight, ("pool", "head"), WEIGHT_MOVES)
    got, oth, weight = lax.optimization_barrier((got, oth, weight))

    span = NY * ROWS
    outer = (x == GROUP_X[0][0]) | (x == GROUP_X[0][1])
    mine = jnp.where(
        outer,
        jnp.concatenate([branch_prefix[xx * span : (xx + 1) * span] for xx in GROUP_X[0]]),
        jnp.concatenate([branch_prefix[xx * span : (xx + 1) * span] for xx in GROUP_X[1]]),
    )
    hide = jnp.where(mine[:, None] == jnp.arange(LANES, dtype=jnp.int32)[None, :], HIDE, 0.0).astype(bf16)

    suffix_numer, suffix_stat = call(
        suffix_kernel,
        (
            jax.ShapeDtypeStruct((ROWS, HEADS * HD), f32),
            jax.ShapeDtypeStruct((ROWS, LANES), f32),
        ),
        queries,
        suffix_len[:, None],
        suffix_keys[0],
        suffix_values[0],
        flops=2 * 2 * 128 * 128 * 4096,
        moved=2 * 2**20,
    )

    state = call(
        owner_kernel,
        jax.ShapeDtypeStruct((MEMBERS, ROWS, HEADS * HD + LANES), bf16),
        got,
        hide,
        own,
        oth,
        flops=4 * 2048 * 2048 * 128,
        moved=2 * 2**20,
        scratch=[pltpu.VMEM((2, prefix_keys.shape[1], 2 * HD), bf16)],
    )
    weight = lax.all_gather(weight, "head", axis=0, tiled=True)
    state = lax.all_to_all(
        state, "pool", split_axis=0, concat_axis=0, tiled=True, axis_index_groups=GROUPS
    )
    attention = call(
        join_kernel,
        jax.ShapeDtypeStruct((ROWS, HEADS * HD), bf16),
        state,
        suffix_numer,
        suffix_stat,
        flops=2**21,
        moved=2**20,
    )

    attention = lax.ppermute(attention, ("pool", "head"), ATTENTION_MOVES)
    blocks = lax.all_to_all(
        jnp.broadcast_to(attention[None], (NY,) + attention.shape),
        "pool",
        split_axis=0,
        concat_axis=0,
        tiled=True,
        axis_index_groups=Y_GROUPS,
    )
    partial = call(
        project_kernel,
        jax.ShapeDtypeStruct((NX, 2 * ROWS, out_weight.shape[1]), bf16),
        blocks,
        weight,
        flops=2 * 64 * 8192 * 256,
        moved=5 * 2**20,
    )
    partial = lax.all_to_all(
        partial, "pool", split_axis=0, concat_axis=0, tiled=True, axis_index_groups=X_GROUPS
    )
    return call(
        sum_kernel,
        jax.ShapeDtypeStruct((2 * ROWS, out_weight.shape[1]), bf16),
        partial,
        flops=2**16,
        moved=2**18,
    )


def solution(mesh):
    in_specs = (
        P("pool", "head"),
        P(),
        P("pool"),
        P("pool"),
        P("head", "pool", None),
        P("head", "pool", None),
        P("head", "pool", None, None),
        P("head", "pool", None, None),
        P("head", "pool"),
    )
    out_specs = P("head", "pool")
    return jax.shard_map(
        on_device, mesh=mesh, in_specs=in_specs, out_specs=out_specs, check_vma=False
    )
```

```python
import math

import jax
import jax.numpy as jnp
from jax import lax
from jax.experimental import pallas as pl
from jax.experimental.pallas import tpu as pltpu
from jax.sharding import PartitionSpec as P

CPP = 16
NX, NY = 4, 8
HEADS = 4
HD = 128
ROWS = 32
MEMBERS = 16
LANES = 128
STATS = 16
TAB = 16
HIDE = -1e30
FLOOR = -262144.0
LOG2E = 1.4426950408889634
SCALE = LOG2E / math.sqrt(HD)
f32, bf16 = jnp.float32, jnp.bfloat16

GROUP_X = ((0, 3), (1, 2))
GROUPS = [[x * NY + y for x in xs for y in range(NY)] for xs in GROUP_X]
PAIR = [(x * NY + y, (x ^ 1) * NY + y) for x in range(NX) for y in range(NY)]
X_GROUPS = [[x * NY + y for x in range(NX)] for y in range(NY)]
Y_GROUPS = [[x * NY + y for y in range(NY)] for x in range(NX)]
NH = 16


def place(x, y, h):
    return (x * NY + y) * NH + h


EVERY = [(x, y, h) for x in range(NX) for y in range(NY) for h in range(NH)]
WEIGHT_MOVES = [(place(x, y, h), place(h % NX, y, h - h % NX + x)) for x, y, h in EVERY]
ATTENTION_MOVES = [
    (place(x, y, h), place(h % NX, (y % 2) * NX + h // NX, NX * x + y // 2)) for x, y, h in EVERY
]


def nt_dot(a, b):
    return lax.dot_general(a, b, (((1,), (1,)), ((), ())), preferred_element_type=f32)


def suffix_kernel(q_ref, len_ref, k_ref, v_ref, numer_ref, stat_ref):
    rows = HEADS * ROWS
    q = jnp.concatenate([q_ref[:, j * HD : (j + 1) * HD] for j in range(HEADS)], axis=0)
    row = lax.broadcasted_iota(jnp.int32, (rows, LANES), 0) % ROWS
    lane = lax.broadcasted_iota(jnp.int32, (rows, LANES), 1)
    live = lane < jnp.concatenate([len_ref[...]] * HEADS, axis=0)
    picked = jnp.full((rows, LANES), HIDE, f32)
    for b in range(ROWS):
        picked = jnp.where(row == b, nt_dot(q, k_ref[b]), picked)
    picked = jnp.where(live, picked, HIDE)
    high = jnp.max(picked, axis=1, keepdims=True)
    weights = jnp.exp2((picked - high) * SCALE)
    totals = jnp.sum(weights, axis=1, keepdims=True)
    rounded = weights.astype(bf16)
    zero = jnp.zeros((rows, LANES), bf16)
    acc = jnp.zeros((rows, HD), f32)
    for b in range(0, ROWS, 2):
        w = jnp.concatenate(
            [jnp.where(row == b, weights, 0.0).astype(bf16), jnp.where(row == b + 1, weights, 0.0).astype(bf16)],
            axis=1,
        )
        v = jnp.concatenate([v_ref[b], v_ref[b + 1]], axis=0)
        acc = acc + jnp.dot(w, v, preferred_element_type=f32)
    for j in range(HEADS):
        numer_ref[:, j * HD : (j + 1) * HD] = acc[j * ROWS : (j + 1) * ROWS]
    lane = lax.broadcasted_iota(jnp.int32, (ROWS, LANES), 1)
    stat = jnp.zeros((ROWS, LANES), f32)
    for j in range(HEADS):
        part = slice(j * ROWS, (j + 1) * ROWS)
        stat = jnp.where(lane == j, high[part] * SCALE, stat)
        stat = jnp.where(lane == HEADS + j, totals[part], stat)
    stat = jnp.concatenate([stat, jnp.zeros((LANES - ROWS, LANES), f32)], axis=0)
    stat_ref[...] = stat.T[: 2 * HEADS]


def keys_kernel(own_ref, oth_ref, keys_ref, values_ref):
    tokens = (own_ref.shape[0] - TAB) // 2
    slots = tokens // LANES
    lane = lax.broadcasted_iota(jnp.int32, (LANES, LANES), 1)
    for o, ref in enumerate((own_ref, oth_ref)):
        table = ref[2 * tokens : 2 * tokens + TAB, :].astype(f32)
        keys_ref[o, :, :HD] = ref[:tokens, :]
        values_ref[o] = ref[tokens : 2 * tokens, :]
        for s in range(slots):
            other = (lane < CPP) & (lane.astype(f32) != table[0:1, s : s + 1])
            keys_ref[o, s * LANES : (s + 1) * LANES, HD:] = jnp.where(other, 1.0, 0.0).astype(bf16)


def owner_kernel(q_ref, hide_ref, keys_ref, values_ref, out_ref):
    branches = MEMBERS * ROWS
    block = 512
    lane = lax.broadcasted_iota(jnp.int32, (block, LANES), 1)
    per = block // ROWS
    unit = jnp.where(
        lax.broadcasted_iota(jnp.int32, (STATS, LANES), 0)
        == lax.broadcasted_iota(jnp.int32, (STATS, LANES), 1),
        1.0,
        0.0,
    ).astype(bf16)
    for r in range(branches // block):
        hide = hide_ref[r * block : (r + 1) * block, :]
        stat = jnp.zeros((block, LANES), f32)
        for j in range(HEADS):
            q = q_ref[r * per : (r + 1) * per, :, j * HD : (j + 1) * HD].reshape(block, HD)
            q = jnp.concatenate([q, hide], axis=1)
            parts = []
            for o in range(keys_ref.shape[0]):
                scores = nt_dot(q, keys_ref[o])
                high = jnp.maximum(jnp.max(scores, axis=1, keepdims=True), FLOOR)
                weights = jnp.exp2((scores - high) * SCALE)
                totals = jnp.sum(weights, axis=1, keepdims=True)
                numer = jnp.dot(weights.astype(bf16), values_ref[o], preferred_element_type=f32)
                parts.append((high * SCALE, totals, numer))
            (ha, ta, na), (hb, tb, nb) = parts
            high = jnp.maximum(ha, hb).astype(bf16).astype(f32)
            fa, fb = jnp.exp2(ha - high), jnp.exp2(hb - high)
            numer = na * fa + nb * fb
            totals = ta * fa + tb * fb
            coarse = totals.astype(bf16).astype(f32)
            out_ref[r * per : (r + 1) * per, j * ROWS : (j + 1) * ROWS, :] = numer.astype(bf16).reshape(per, ROWS, HD)
            stat = jnp.where(lane == j, high, stat)
            stat = jnp.where(lane == HEADS + j, coarse, stat)
            stat = jnp.where(lane == 2 * HEADS + j, totals - coarse, stat)
        stat = stat.astype(bf16)
        for i in range(per):
            turned = nt_dot(unit, stat[i * ROWS : (i + 1) * ROWS])
            out_ref[r * per + i, HEADS * ROWS :, :ROWS] = turned.astype(bf16)


def join_kernel(got_ref, numer_ref, stat_ref, out_ref):
    own = stat_ref[...]
    wide = HEADS * ROWS
    stats = [got_ref[i, wide:, :].astype(f32) for i in range(MEMBERS)]
    top = own[:HEADS]
    for stat in stats:
        top = jnp.maximum(top, stat[:HEADS])
    factors = [jnp.exp2(own[:HEADS] - top)]
    total = own[HEADS:] * factors[0]
    for stat in stats:
        factors.append(jnp.exp2(stat[:HEADS] - top))
        total = total + (stat[HEADS : 2 * HEADS] + stat[2 * HEADS : 3 * HEADS]) * factors[-1]
    inverse = 1.0 / total
    rows = jnp.concatenate([f * inverse for f in factors], axis=0)
    rows = jnp.concatenate([rows, jnp.zeros((LANES - rows.shape[0], LANES), f32)], axis=0)
    columns = rows.T[:ROWS]
    for j in range(HEADS):
        acc = numer_ref[:, j * HD : (j + 1) * HD] * columns[:, j : j + 1]
        for i in range(MEMBERS):
            at = (i + 1) * HEADS + j
            acc = acc + got_ref[i, j * ROWS : (j + 1) * ROWS, :].astype(f32) * columns[:, at : at + 1]
        out_ref[:, j * HD : (j + 1) * HD] = acc.astype(bf16)


def project_kernel(att_ref, w_ref, out_ref):
    depth = att_ref.shape[2]
    half = att_ref.shape[0] // 2
    for c in range(out_ref.shape[0]):
        acc = jnp.zeros(out_ref.shape[1:], f32)
        for k in range(half):
            rows = jnp.concatenate([att_ref[k], att_ref[half + k]], axis=0)
            i = k * out_ref.shape[0] + c
            acc = acc + jnp.dot(rows, w_ref[i * depth : (i + 1) * depth, :], preferred_element_type=f32)
        out_ref[c] = acc.astype(out_ref.dtype)


def sum_kernel(part_ref, out_ref):
    acc = part_ref[0].astype(f32)
    for c in range(1, part_ref.shape[0]):
        acc = acc + part_ref[c].astype(f32)
    out_ref[...] = acc.astype(bf16)


def call(kernel, out_shape, *args, flops=0, moved=0):
    return pl.pallas_call(
        kernel,
        out_shape=out_shape,
        compiler_params=pltpu.CompilerParams(vmem_limit_bytes=40 * 2**20),
        cost_estimate=pl.CostEstimate(flops=flops, bytes_accessed=moved, transcendentals=0),
    )(*args)


def after(value, other):
    return lax.optimization_barrier((value, other))[0]


def on_device(
    queries,
    branch_prefix,
    stretch_table,
    suffix_len,
    prefix_keys,
    prefix_values,
    suffix_keys,
    suffix_values,
    out_weight,
):
    pool = lax.axis_index("pool")
    x = pool // NY
    slots = stretch_table.shape[0]

    prefixes = (stretch_table // CPP).astype(bf16)
    table = jnp.zeros((TAB, LANES), bf16).at[0, :slots].set(prefixes)
    own = jnp.concatenate([prefix_keys[0], prefix_values[0], table], axis=0)
    oth = lax.ppermute(own, "pool", PAIR)

    got = lax.all_to_all(
        jnp.broadcast_to(queries[None], (MEMBERS,) + queries.shape),
        "pool",
        split_axis=0,
        concat_axis=0,
        tiled=True,
        axis_index_groups=GROUPS,
    )
    weight = lax.ppermute(out_weight, ("pool", "head"), WEIGHT_MOVES)
    keys, values = call(
        keys_kernel,
        (
            jax.ShapeDtypeStruct((2, prefix_keys.shape[1], 2 * HD), bf16),
            jax.ShapeDtypeStruct((2, prefix_keys.shape[1], HD), bf16),
        ),
        own,
        oth,
        flops=20 * 2**30,
        moved=2 * 2**20,
    )
    got, weight, keys, values = lax.optimization_barrier((got, weight, keys, values))
    weight = lax.all_gather(weight, "head", axis=0, tiled=True)

    span = NY * ROWS
    outer = (x == GROUP_X[0][0]) | (x == GROUP_X[0][1])
    mine = jnp.where(
        outer,
        jnp.concatenate([branch_prefix[xx * span : (xx + 1) * span] for xx in GROUP_X[0]]),
        jnp.concatenate([branch_prefix[xx * span : (xx + 1) * span] for xx in GROUP_X[1]]),
    )
    hide = jnp.where(mine[:, None] == jnp.arange(LANES, dtype=jnp.int32)[None, :], HIDE, 0.0).astype(bf16)

    suffix_numer, suffix_stat = call(
        suffix_kernel,
        (
            jax.ShapeDtypeStruct((ROWS, HEADS * HD), f32),
            jax.ShapeDtypeStruct((2 * HEADS, LANES), f32),
        ),
        queries,
        suffix_len[:, None],
        suffix_keys[0],
        suffix_values[0],
        flops=2 * 2 * 128 * 128 * 4096,
        moved=2 * 2**20,
    )

    state = call(
        owner_kernel,
        jax.ShapeDtypeStruct((MEMBERS, HEADS * ROWS + STATS, HD), bf16),
        got,
        hide,
        keys,
        values,
        flops=4 * 2048 * 2048 * 128,
        moved=2 * 2**20,
    )
    state = lax.all_to_all(
        state, "pool", split_axis=0, concat_axis=0, tiled=True, axis_index_groups=GROUPS
    )
    attention = call(
        join_kernel,
        jax.ShapeDtypeStruct((ROWS, HEADS * HD), bf16),
        state,
        suffix_numer,
        suffix_stat,
        flops=2**21,
        moved=2**20,
    )

    attention = lax.ppermute(attention, ("pool", "head"), ATTENTION_MOVES)
    blocks = lax.all_to_all(
        jnp.broadcast_to(attention[None], (NY,) + attention.shape),
        "pool",
        split_axis=0,
        concat_axis=0,
        tiled=True,
        axis_index_groups=Y_GROUPS,
    )
    partial = call(
        project_kernel,
        jax.ShapeDtypeStruct((NX, 2 * ROWS, out_weight.shape[1]), bf16),
        blocks,
        weight,
        flops=2 * 64 * 8192 * 256,
        moved=5 * 2**20,
    )
    partial = lax.all_to_all(
        partial, "pool", split_axis=0, concat_axis=0, tiled=True, axis_index_groups=X_GROUPS
    )
    return call(
        sum_kernel,
        jax.ShapeDtypeStruct((2 * ROWS, out_weight.shape[1]), bf16),
        partial,
        flops=2**16,
        moved=2**18,
    )


def solution(mesh):
    in_specs = (
        P("pool", "head"),
        P(),
        P("pool"),
        P("pool"),
        P("head", "pool", None),
        P("head", "pool", None),
        P("head", "pool", None, None),
        P("head", "pool", None, None),
        P("head", "pool"),
    )
    out_specs = P("head", "pool")
    return jax.shard_map(
        on_device, mesh=mesh, in_specs=in_specs, out_specs=out_specs, check_vma=False
    )
```

```python
import math

import jax
import jax.numpy as jnp
from jax import lax
from jax.experimental import pallas as pl
from jax.experimental.pallas import tpu as pltpu
from jax.sharding import PartitionSpec as P

CPP = 16
NX, NY = 4, 8
HEADS = 4
HD = 128
ROWS = 32
MEMBERS = 16
LANES = 128
STATS = 16
TAB = 16
HIDE = -1e30
FLOOR = -262144.0
LOG2E = 1.4426950408889634
SCALE = LOG2E / math.sqrt(HD)
f32, bf16 = jnp.float32, jnp.bfloat16

GROUP_X = ((0, 3), (1, 2))
GROUPS = [[x * NY + y for x in xs for y in range(NY)] for xs in GROUP_X]
PAIR = [(x * NY + y, (x ^ 1) * NY + y) for x in range(NX) for y in range(NY)]
X_GROUPS = [[x * NY + y for x in range(NX)] for y in range(NY)]
Y_GROUPS = [[x * NY + y for y in range(NY)] for x in range(NX)]
NH = 16


def place(x, y, h):
    return (x * NY + y) * NH + h


EVERY = [(x, y, h) for x in range(NX) for y in range(NY) for h in range(NH)]
WEIGHT_MOVES = [(place(x, y, h), place(h % NX, y, h - h % NX + x)) for x, y, h in EVERY]
ATTENTION_MOVES = [
    (
        place(x, y, h),
        place(h % NX, (y + h // NX if y % 2 else y - h // NX) % NY, NX * x + y // 2),
    )
    for x, y, h in EVERY
]


def nt_dot(a, b):
    return lax.dot_general(a, b, (((1,), (1,)), ((), ())), preferred_element_type=f32)


def suffix_kernel(q_ref, len_ref, k_ref, v_ref, numer_ref, stat_ref):
    rows = HEADS * ROWS
    q = jnp.concatenate([q_ref[:, j * HD : (j + 1) * HD] for j in range(HEADS)], axis=0)
    row = lax.broadcasted_iota(jnp.int32, (rows, LANES), 0) % ROWS
    lane = lax.broadcasted_iota(jnp.int32, (rows, LANES), 1)
    live = lane < jnp.concatenate([len_ref[...]] * HEADS, axis=0)
    picked = jnp.full((rows, LANES), HIDE, f32)
    for b in range(ROWS):
        picked = jnp.where(row == b, nt_dot(q, k_ref[b]), picked)
    picked = jnp.where(live, picked, HIDE)
    high = jnp.max(picked, axis=1, keepdims=True)
    weights = jnp.exp2((picked - high) * SCALE)
    totals = jnp.sum(weights, axis=1, keepdims=True)
    rounded = weights.astype(bf16)
    zero = jnp.zeros((rows, LANES), bf16)
    acc = jnp.zeros((rows, HD), f32)
    for b in range(0, ROWS, 2):
        w = jnp.concatenate(
            [jnp.where(row == b, weights, 0.0).astype(bf16), jnp.where(row == b + 1, weights, 0.0).astype(bf16)],
            axis=1,
        )
        v = jnp.concatenate([v_ref[b], v_ref[b + 1]], axis=0)
        acc = acc + jnp.dot(w, v, preferred_element_type=f32)
    for j in range(HEADS):
        numer_ref[:, j * HD : (j + 1) * HD] = acc[j * ROWS : (j + 1) * ROWS]
    lane = lax.broadcasted_iota(jnp.int32, (ROWS, LANES), 1)
    stat = jnp.zeros((ROWS, LANES), f32)
    for j in range(HEADS):
        part = slice(j * ROWS, (j + 1) * ROWS)
        stat = jnp.where(lane == j, high[part] * SCALE, stat)
        stat = jnp.where(lane == HEADS + j, totals[part], stat)
    stat = jnp.concatenate([stat, jnp.zeros((LANES - ROWS, LANES), f32)], axis=0)
    stat_ref[...] = stat.T[: 2 * HEADS]


def keys_kernel(own_ref, oth_ref, keys_ref, values_ref):
    tokens = (own_ref.shape[0] - TAB) // 2
    slots = tokens // LANES
    lane = lax.broadcasted_iota(jnp.int32, (LANES, LANES), 1)
    for o, ref in enumerate((own_ref, oth_ref)):
        table = ref[2 * tokens : 2 * tokens + TAB, :].astype(f32)
        keys_ref[o, :, :HD] = ref[:tokens, :]
        values_ref[o] = ref[tokens : 2 * tokens, :]
        for s in range(slots):
            other = (lane < CPP) & (lane.astype(f32) != table[0:1, s : s + 1])
            keys_ref[o, s * LANES : (s + 1) * LANES, HD:] = jnp.where(other, 1.0, 0.0).astype(bf16)


def owner_kernel(q_ref, hide_ref, keys_ref, values_ref, out_ref):
    branches = MEMBERS * ROWS
    block = 512
    lane = lax.broadcasted_iota(jnp.int32, (block, LANES), 1)
    per = block // ROWS
    unit = jnp.where(
        lax.broadcasted_iota(jnp.int32, (STATS, LANES), 0)
        == lax.broadcasted_iota(jnp.int32, (STATS, LANES), 1),
        1.0,
        0.0,
    ).astype(bf16)
    for r in range(branches // block):
        hide = hide_ref[r * block : (r + 1) * block, :]
        stat = jnp.zeros((block, LANES), f32)
        for j in range(HEADS):
            q = q_ref[r * per : (r + 1) * per, :, j * HD : (j + 1) * HD].reshape(block, HD)
            q = jnp.concatenate([q, hide], axis=1)
            parts = []
            for o in range(keys_ref.shape[0]):
                scores = nt_dot(q, keys_ref[o])
                high = jnp.maximum(jnp.max(scores, axis=1, keepdims=True), FLOOR)
                weights = jnp.exp2((scores - high) * SCALE)
                totals = jnp.sum(weights, axis=1, keepdims=True)
                numer = jnp.dot(weights.astype(bf16), values_ref[o], preferred_element_type=f32)
                parts.append((high * SCALE, totals, numer))
            (ha, ta, na), (hb, tb, nb) = parts
            high = jnp.maximum(ha, hb).astype(bf16).astype(f32)
            fa, fb = jnp.exp2(ha - high), jnp.exp2(hb - high)
            numer = na * fa + nb * fb
            totals = ta * fa + tb * fb
            coarse = totals.astype(bf16).astype(f32)
            out_ref[r * per : (r + 1) * per, j * ROWS : (j + 1) * ROWS, :] = numer.astype(bf16).reshape(per, ROWS, HD)
            stat = jnp.where(lane == j, high, stat)
            stat = jnp.where(lane == HEADS + j, coarse, stat)
            stat = jnp.where(lane == 2 * HEADS + j, totals - coarse, stat)
        stat = stat.astype(bf16)
        for i in range(per):
            turned = nt_dot(unit, stat[i * ROWS : (i + 1) * ROWS])
            out_ref[r * per + i, HEADS * ROWS :, :ROWS] = turned.astype(bf16)


def join_kernel(got_ref, numer_ref, stat_ref, out_ref):
    own = stat_ref[...]
    wide = HEADS * ROWS
    stats = [got_ref[i, wide:, :].astype(f32) for i in range(MEMBERS)]
    top = own[:HEADS]
    for stat in stats:
        top = jnp.maximum(top, stat[:HEADS])
    factors = [jnp.exp2(own[:HEADS] - top)]
    total = own[HEADS:] * factors[0]
    for stat in stats:
        factors.append(jnp.exp2(stat[:HEADS] - top))
        total = total + (stat[HEADS : 2 * HEADS] + stat[2 * HEADS : 3 * HEADS]) * factors[-1]
    inverse = 1.0 / total
    rows = jnp.concatenate([f * inverse for f in factors], axis=0)
    rows = jnp.concatenate([rows, jnp.zeros((LANES - rows.shape[0], LANES), f32)], axis=0)
    columns = rows.T[:ROWS]
    for j in range(HEADS):
        acc = numer_ref[:, j * HD : (j + 1) * HD] * columns[:, j : j + 1]
        for i in range(MEMBERS):
            at = (i + 1) * HEADS + j
            acc = acc + got_ref[i, j * ROWS : (j + 1) * ROWS, :].astype(f32) * columns[:, at : at + 1]
        out_ref[:, j * HD : (j + 1) * HD] = acc.astype(bf16)


def project_kernel(first_ref, att_ref, w_ref, out_ref):
    depth = att_ref.shape[2]
    half = att_ref.shape[0] // 2
    first = first_ref[0]
    for c in range(out_ref.shape[0]):
        acc = jnp.zeros(out_ref.shape[1:], f32)
        for k in range(half):
            down, up = (first + NY - k) % NY, (first + 1 + k) % NY
            rows = jnp.concatenate([att_ref[down], att_ref[up]], axis=0)
            i = k * out_ref.shape[0] + c
            acc = acc + jnp.dot(rows, w_ref[i * depth : (i + 1) * depth, :], preferred_element_type=f32)
        out_ref[c] = acc.astype(out_ref.dtype)


def sum_kernel(part_ref, out_ref):
    acc = part_ref[0].astype(f32)
    for c in range(1, part_ref.shape[0]):
        acc = acc + part_ref[c].astype(f32)
    out_ref[...] = acc.astype(bf16)


def call(kernel, out_shape, *args, flops=0, moved=0):
    return pl.pallas_call(
        kernel,
        out_shape=out_shape,
        compiler_params=pltpu.CompilerParams(vmem_limit_bytes=40 * 2**20),
        cost_estimate=pl.CostEstimate(flops=flops, bytes_accessed=moved, transcendentals=0),
    )(*args)


def after(value, other):
    return lax.optimization_barrier((value, other))[0]


def on_device(
    queries,
    branch_prefix,
    stretch_table,
    suffix_len,
    prefix_keys,
    prefix_values,
    suffix_keys,
    suffix_values,
    out_weight,
):
    pool = lax.axis_index("pool")
    x = pool // NY
    slots = stretch_table.shape[0]

    prefixes = (stretch_table // CPP).astype(bf16)
    table = jnp.zeros((TAB, LANES), bf16).at[0, :slots].set(prefixes)
    own = jnp.concatenate([prefix_keys[0], prefix_values[0], table], axis=0)
    oth = lax.ppermute(own, "pool", PAIR)

    got = lax.all_to_all(
        jnp.broadcast_to(queries[None], (MEMBERS,) + queries.shape),
        "pool",
        split_axis=0,
        concat_axis=0,
        tiled=True,
        axis_index_groups=GROUPS,
    )
    weight = lax.ppermute(out_weight, ("pool", "head"), WEIGHT_MOVES)
    keys, values = call(
        keys_kernel,
        (
            jax.ShapeDtypeStruct((2, prefix_keys.shape[1], 2 * HD), bf16),
            jax.ShapeDtypeStruct((2, prefix_keys.shape[1], HD), bf16),
        ),
        own,
        oth,
        flops=20 * 2**30,
        moved=2 * 2**20,
    )
    got, weight, keys, values = lax.optimization_barrier((got, weight, keys, values))

    span = NY * ROWS
    outer = (x == GROUP_X[0][0]) | (x == GROUP_X[0][1])
    mine = jnp.where(
        outer,
        jnp.concatenate([branch_prefix[xx * span : (xx + 1) * span] for xx in GROUP_X[0]]),
        jnp.concatenate([branch_prefix[xx * span : (xx + 1) * span] for xx in GROUP_X[1]]),
    )
    hide = jnp.where(mine[:, None] == jnp.arange(LANES, dtype=jnp.int32)[None, :], HIDE, 0.0).astype(bf16)

    suffix_numer, suffix_stat = call(
        suffix_kernel,
        (
            jax.ShapeDtypeStruct((ROWS, HEADS * HD), f32),
            jax.ShapeDtypeStruct((2 * HEADS, LANES), f32),
        ),
        queries,
        suffix_len[:, None],
        suffix_keys[0],
        suffix_values[0],
        flops=2 * 2 * 128 * 128 * 4096,
        moved=2 * 2**20,
    )

    state = call(
        owner_kernel,
        jax.ShapeDtypeStruct((MEMBERS, HEADS * ROWS + STATS, HD), bf16),
        got,
        hide,
        keys,
        values,
        flops=4 * 2048 * 2048 * 128,
        moved=2 * 2**20,
    )
    state, weight = lax.optimization_barrier((state, weight))
    weight = lax.all_gather(weight, "head", axis=0, tiled=True)
    state = lax.all_to_all(
        state, "pool", split_axis=0, concat_axis=0, tiled=True, axis_index_groups=GROUPS
    )
    attention = call(
        join_kernel,
        jax.ShapeDtypeStruct((ROWS, HEADS * HD), bf16),
        state,
        suffix_numer,
        suffix_stat,
        flops=2**21,
        moved=2**20,
    )

    attention = lax.ppermute(attention, ("pool", "head"), ATTENTION_MOVES)
    blocks = lax.all_to_all(
        jnp.broadcast_to(attention[None], (NY,) + attention.shape),
        "pool",
        split_axis=0,
        concat_axis=0,
        tiled=True,
        axis_index_groups=Y_GROUPS,
    )
    vmem = pl.BlockSpec(memory_space=pltpu.VMEM)
    partial = pl.pallas_call(
        project_kernel,
        out_shape=jax.ShapeDtypeStruct((NX, 2 * ROWS, out_weight.shape[1]), bf16),
        in_specs=[pl.BlockSpec(memory_space=pltpu.SMEM), vmem, vmem],
        out_specs=vmem,
        compiler_params=pltpu.CompilerParams(vmem_limit_bytes=40 * 2**20),
        cost_estimate=pl.CostEstimate(
            flops=2 * 64 * 8192 * 256, bytes_accessed=5 * 2**20, transcendentals=0
        ),
    )((lax.axis_index("head") % NX * 2)[None], blocks, weight)
    partial = lax.all_to_all(
        partial, "pool", split_axis=0, concat_axis=0, tiled=True, axis_index_groups=X_GROUPS
    )
    return call(
        sum_kernel,
        jax.ShapeDtypeStruct((2 * ROWS, out_weight.shape[1]), bf16),
        partial,
        flops=2**16,
        moved=2**18,
    )


def solution(mesh):
    in_specs = (
        P("pool", "head"),
        P(),
        P("pool"),
        P("pool"),
        P("head", "pool", None),
        P("head", "pool", None),
        P("head", "pool", None, None),
        P("head", "pool", None, None),
        P("head", "pool"),
    )
    out_specs = P("head", "pool")
    return jax.shard_map(
        on_device, mesh=mesh, in_specs=in_specs, out_specs=out_specs, check_vma=False
    )
```

```python
import math

import jax
import jax.numpy as jnp
from jax import lax
from jax.experimental import pallas as pl
from jax.experimental.pallas import tpu as pltpu
from jax.sharding import PartitionSpec as P

CPP = 16
NX, NY = 4, 8
HEADS = 4
HD = 128
ROWS = 32
MEMBERS = 16
LANES = 128
STATS = 16
TAB = 16
HIDE = -1e30
FLOOR = -262144.0
LOG2E = 1.4426950408889634
SCALE = LOG2E / math.sqrt(HD)
f32, bf16 = jnp.float32, jnp.bfloat16

GROUP_X = ((0, 3), (1, 2))
GROUPS = [[x * NY + y for x in xs for y in range(NY)] for xs in GROUP_X]
PAIR = [(x * NY + y, (x ^ 1) * NY + y) for x in range(NX) for y in range(NY)]
X_GROUPS = [[x * NY + y for x in range(NX)] for y in range(NY)]
Y_GROUPS = [[x * NY + y for y in range(NY)] for x in range(NX)]
NH = 16


def place(x, y, h):
    return (x * NY + y) * NH + h


EVERY = [(x, y, h) for x in range(NX) for y in range(NY) for h in range(NH)]
WEIGHT_MOVES = [(place(x, y, h), place(h % NX, y, h - h % NX + x)) for x, y, h in EVERY]
ATTENTION_MOVES = [
    (
        place(x, y, h),
        place(h % NX, (y + h // NX if y % 2 else y - h // NX) % NY, NX * x + y // 2),
    )
    for x, y, h in EVERY
]


def nt_dot(a, b):
    return lax.dot_general(a, b, (((1,), (1,)), ((), ())), preferred_element_type=f32)


def suffix_kernel(q_ref, len_ref, k_ref, v_ref, numer_ref, stat_ref):
    rows = HEADS * ROWS
    q = jnp.concatenate([q_ref[:, j * HD : (j + 1) * HD] for j in range(HEADS)], axis=0)
    row = lax.broadcasted_iota(jnp.int32, (rows, LANES), 0) % ROWS
    lane = lax.broadcasted_iota(jnp.int32, (rows, LANES), 1)
    live = lane < jnp.concatenate([len_ref[...]] * HEADS, axis=0)
    picked = jnp.full((rows, LANES), HIDE, f32)
    for b in range(ROWS):
        picked = jnp.where(row == b, nt_dot(q, k_ref[b]), picked)
    picked = jnp.where(live, picked, HIDE)
    high = jnp.max(picked, axis=1, keepdims=True)
    weights = jnp.exp2((picked - high) * SCALE)
    totals = jnp.sum(weights, axis=1, keepdims=True)
    rounded = weights.astype(bf16)
    zero = jnp.zeros((rows, LANES), bf16)
    acc = jnp.zeros((rows, HD), f32)
    for b in range(0, ROWS, 2):
        w = jnp.concatenate(
            [jnp.where(row == b, weights, 0.0).astype(bf16), jnp.where(row == b + 1, weights, 0.0).astype(bf16)],
            axis=1,
        )
        v = jnp.concatenate([v_ref[b], v_ref[b + 1]], axis=0)
        acc = acc + jnp.dot(w, v, preferred_element_type=f32)
    for j in range(HEADS):
        numer_ref[:, j * HD : (j + 1) * HD] = acc[j * ROWS : (j + 1) * ROWS]
    lane = lax.broadcasted_iota(jnp.int32, (ROWS, LANES), 1)
    stat = jnp.zeros((ROWS, LANES), f32)
    for j in range(HEADS):
        part = slice(j * ROWS, (j + 1) * ROWS)
        stat = jnp.where(lane == j, high[part] * SCALE, stat)
        stat = jnp.where(lane == HEADS + j, totals[part], stat)
    stat = jnp.concatenate([stat, jnp.zeros((LANES - ROWS, LANES), f32)], axis=0)
    stat_ref[...] = stat.T[: 2 * HEADS]


def keys_kernel(own_ref, oth_ref, keys_ref, values_ref):
    tokens = (own_ref.shape[0] - TAB) // 2
    slots = tokens // LANES
    lane = lax.broadcasted_iota(jnp.int32, (LANES, LANES), 1)
    for o, ref in enumerate((own_ref, oth_ref)):
        table = ref[2 * tokens : 2 * tokens + TAB, :].astype(f32)
        keys_ref[o, :, :HD] = ref[:tokens, :]
        values_ref[o] = ref[tokens : 2 * tokens, :]
        for s in range(slots):
            other = (lane < CPP) & (lane.astype(f32) != table[0:1, s : s + 1])
            keys_ref[o, s * LANES : (s + 1) * LANES, HD:] = jnp.where(other, 1.0, 0.0).astype(bf16)


def owner_kernel(q_ref, hide_ref, keys_ref, values_ref, out_ref):
    branches = MEMBERS * ROWS
    block = 512
    lane = lax.broadcasted_iota(jnp.int32, (block, LANES), 1)
    per = block // ROWS
    unit = jnp.where(
        lax.broadcasted_iota(jnp.int32, (STATS, LANES), 0)
        == lax.broadcasted_iota(jnp.int32, (STATS, LANES), 1),
        1.0,
        0.0,
    ).astype(bf16)
    for r in range(branches // block):
        hide = hide_ref[r * block : (r + 1) * block, :]
        stat = jnp.zeros((block, LANES), f32)
        for j in range(HEADS):
            q = q_ref[r * per : (r + 1) * per, :, j * HD : (j + 1) * HD].reshape(block, HD)
            q = jnp.concatenate([q, hide], axis=1)
            parts = []
            for o in range(keys_ref.shape[0]):
                scores = nt_dot(q, keys_ref[o])
                high = jnp.maximum(jnp.max(scores, axis=1, keepdims=True), FLOOR)
                weights = jnp.exp2((scores - high) * SCALE)
                totals = jnp.sum(weights, axis=1, keepdims=True)
                numer = jnp.dot(weights.astype(bf16), values_ref[o], preferred_element_type=f32)
                parts.append((high * SCALE, totals, numer))
            (ha, ta, na), (hb, tb, nb) = parts
            high = jnp.maximum(ha, hb).astype(bf16).astype(f32)
            fa, fb = jnp.exp2(ha - high), jnp.exp2(hb - high)
            numer = na * fa + nb * fb
            totals = ta * fa + tb * fb
            coarse = totals.astype(bf16).astype(f32)
            out_ref[r * per : (r + 1) * per, j * ROWS : (j + 1) * ROWS, :] = numer.astype(bf16).reshape(per, ROWS, HD)
            stat = jnp.where(lane == j, high, stat)
            stat = jnp.where(lane == HEADS + j, coarse, stat)
            stat = jnp.where(lane == 2 * HEADS + j, totals - coarse, stat)
        stat = stat.astype(bf16)
        for i in range(per):
            turned = nt_dot(unit, stat[i * ROWS : (i + 1) * ROWS])
            out_ref[r * per + i, HEADS * ROWS :, :ROWS] = turned.astype(bf16)


def join_kernel(got_ref, numer_ref, stat_ref, out_ref):
    own = stat_ref[...]
    wide = HEADS * ROWS
    stats = [got_ref[i, wide:, :].astype(f32) for i in range(MEMBERS)]
    top = own[:HEADS]
    for stat in stats:
        top = jnp.maximum(top, stat[:HEADS])
    factors = [jnp.exp2(own[:HEADS] - top)]
    total = own[HEADS:] * factors[0]
    for stat in stats:
        factors.append(jnp.exp2(stat[:HEADS] - top))
        total = total + (stat[HEADS : 2 * HEADS] + stat[2 * HEADS : 3 * HEADS]) * factors[-1]
    inverse = 1.0 / total
    rows = jnp.concatenate([f * inverse for f in factors], axis=0)
    rows = jnp.concatenate([rows, jnp.zeros((LANES - rows.shape[0], LANES), f32)], axis=0)
    columns = rows.T[:ROWS]
    for j in range(HEADS):
        acc = numer_ref[:, j * HD : (j + 1) * HD] * columns[:, j : j + 1]
        for i in range(MEMBERS):
            at = (i + 1) * HEADS + j
            acc = acc + got_ref[i, j * ROWS : (j + 1) * ROWS, :].astype(f32) * columns[:, at : at + 1]
        out_ref[:, j * HD : (j + 1) * HD] = acc.astype(bf16)


def project_kernel(first_ref, att_ref, w_ref, out_ref):
    depth = att_ref.shape[2]
    half = att_ref.shape[0] // 2
    first = first_ref[0]
    for c in range(out_ref.shape[0]):
        acc = jnp.zeros(out_ref.shape[1:], f32)
        for k in range(half):
            down, up = (first + NY - k) % NY, (first + 1 + k) % NY
            rows = jnp.concatenate([att_ref[down], att_ref[up]], axis=0)
            i = k * out_ref.shape[0] + c
            acc = acc + jnp.dot(rows, w_ref[i * depth : (i + 1) * depth, :], preferred_element_type=f32)
        out_ref[c] = acc.astype(out_ref.dtype)


def sum_kernel(part_ref, out_ref):
    acc = part_ref[0].astype(f32)
    for c in range(1, part_ref.shape[0]):
        acc = acc + part_ref[c].astype(f32)
    out_ref[...] = acc.astype(bf16)


def call(kernel, out_shape, *args, flops=0, moved=0):
    return pl.pallas_call(
        kernel,
        out_shape=out_shape,
        compiler_params=pltpu.CompilerParams(vmem_limit_bytes=40 * 2**20),
        cost_estimate=pl.CostEstimate(flops=flops, bytes_accessed=moved, transcendentals=0),
    )(*args)


def after(value, other):
    return lax.optimization_barrier((value, other))[0]


def on_device(
    queries,
    branch_prefix,
    stretch_table,
    suffix_len,
    prefix_keys,
    prefix_values,
    suffix_keys,
    suffix_values,
    out_weight,
):
    pool = lax.axis_index("pool")
    x = pool // NY
    slots = stretch_table.shape[0]

    prefixes = (stretch_table // CPP).astype(bf16)
    table = jnp.zeros((TAB, LANES), bf16).at[0, :slots].set(prefixes)
    own = jnp.concatenate([prefix_keys[0], prefix_values[0], table], axis=0)
    oth = lax.ppermute(own, "pool", PAIR)

    got = lax.all_to_all(
        jnp.broadcast_to(queries[None], (MEMBERS,) + queries.shape),
        "pool",
        split_axis=0,
        concat_axis=0,
        tiled=True,
        axis_index_groups=GROUPS,
    )
    weight = lax.ppermute(out_weight, ("pool", "head"), WEIGHT_MOVES)
    keys, values = call(
        keys_kernel,
        (
            jax.ShapeDtypeStruct((2, prefix_keys.shape[1], 2 * HD), bf16),
            jax.ShapeDtypeStruct((2, prefix_keys.shape[1], HD), bf16),
        ),
        own,
        oth,
        flops=20 * 2**30,
        moved=2 * 2**20,
    )
    got, weight, keys, values = lax.optimization_barrier((got, weight, keys, values))
    weight = lax.all_gather(weight, "head", axis=0, tiled=True)

    span = NY * ROWS
    outer = (x == GROUP_X[0][0]) | (x == GROUP_X[0][1])
    mine = jnp.where(
        outer,
        jnp.concatenate([branch_prefix[xx * span : (xx + 1) * span] for xx in GROUP_X[0]]),
        jnp.concatenate([branch_prefix[xx * span : (xx + 1) * span] for xx in GROUP_X[1]]),
    )
    hide = jnp.where(mine[:, None] == jnp.arange(LANES, dtype=jnp.int32)[None, :], HIDE, 0.0).astype(bf16)

    suffix_numer, suffix_stat = call(
        suffix_kernel,
        (
            jax.ShapeDtypeStruct((ROWS, HEADS * HD), f32),
            jax.ShapeDtypeStruct((2 * HEADS, LANES), f32),
        ),
        queries,
        suffix_len[:, None],
        suffix_keys[0],
        suffix_values[0],
        flops=2 * 2 * 128 * 128 * 4096,
        moved=2 * 2**20,
    )

    state = call(
        owner_kernel,
        jax.ShapeDtypeStruct((MEMBERS, HEADS * ROWS + STATS, HD), bf16),
        got,
        hide,
        keys,
        values,
        flops=4 * 2048 * 2048 * 128,
        moved=2 * 2**20,
    )
    state = lax.all_to_all(
        state, "pool", split_axis=0, concat_axis=0, tiled=True, axis_index_groups=GROUPS
    )
    attention = call(
        join_kernel,
        jax.ShapeDtypeStruct((ROWS, HEADS * HD), bf16),
        state,
        suffix_numer,
        suffix_stat,
        flops=2**21,
        moved=2**20,
    )

    attention = lax.ppermute(attention, ("pool", "head"), ATTENTION_MOVES)
    blocks = lax.all_to_all(
        jnp.broadcast_to(attention[None], (NY,) + attention.shape),
        "pool",
        split_axis=0,
        concat_axis=0,
        tiled=True,
        axis_index_groups=Y_GROUPS,
    )
    vmem = pl.BlockSpec(memory_space=pltpu.VMEM)
    partial = pl.pallas_call(
        project_kernel,
        out_shape=jax.ShapeDtypeStruct((NX, 2 * ROWS, out_weight.shape[1]), bf16),
        in_specs=[pl.BlockSpec(memory_space=pltpu.SMEM), vmem, vmem],
        out_specs=vmem,
        compiler_params=pltpu.CompilerParams(vmem_limit_bytes=40 * 2**20),
        cost_estimate=pl.CostEstimate(
            flops=2 * 64 * 8192 * 256, bytes_accessed=5 * 2**20, transcendentals=0
        ),
    )((lax.axis_index("head") % NX * 2)[None], blocks, weight)
    partial = lax.all_to_all(
        partial, "pool", split_axis=0, concat_axis=0, tiled=True, axis_index_groups=X_GROUPS
    )
    return call(
        sum_kernel,
        jax.ShapeDtypeStruct((2 * ROWS, out_weight.shape[1]), bf16),
        partial,
        flops=2**16,
        moved=2**18,
    )


def solution(mesh):
    in_specs = (
        P("pool", "head"),
        P(),
        P("pool"),
        P("pool"),
        P("head", "pool", None),
        P("head", "pool", None),
        P("head", "pool", None, None),
        P("head", "pool", None, None),
        P("head", "pool"),
    )
    out_specs = P("head", "pool")
    return jax.shard_map(
        on_device, mesh=mesh, in_specs=in_specs, out_specs=out_specs, check_vma=False
    )
```
